32 devices in a mesh: dp: 4 (over y, x), ctx: 4 (over z), tp: 2 (over core).
Axes of the slice: x: 2, y: 2, z: 4, core: 2. Of those that a mesh axis runs over, the one named last changes fastest.
Arguments:
- cotangent: bfloat16 [6144, 4096], P(('dp', 'ctx')), may hold values from -6 to 6
- gate_pre: bfloat16 [6144, 16384], P(('dp', 'ctx'), 'tp'), may hold values from -6 to 6
- up_pre: bfloat16 [6144, 16384], P(('dp', 'ctx'), 'tp'), may hold values from -6 to 6
- w_down: bfloat16 [4096, 16384], P(('dp', 'ctx'), 'tp'), may hold values from -0.046875 to 0.046875
Outputs:
- grad_gate: bfloat16 [6144, 16384], P(('dp', 'ctx'), 'tp')
- grad_up: bfloat16 [6144, 16384], P(('dp', 'ctx'), 'tp')
- grad_down: bfloat16 [4096, 16384], P(('dp', 'ctx'), 'tp')
The draws below stay inside these ranges and needn't reach their ends.
All inputs are finite; a program needn't handle non-finite values.
Results may differ from the reference program's by a relative error of at most 0.018.
Values may be sent and summed in bfloat16 or wider, within the bound.
A program may use at most 192 MiB of HBM per device.

```python
import jax
import jax.numpy as jnp
from jax import lax

D = 4096
FF = 16384
ROWS = 384
GROUPS = 16
TOKENS = 6144


def raised(values, rng, source, target, blocks, factor):
    owner, partner = [(jnp.arange(values.shape[axis_at]) // (values.shape[axis_at] // blocks)).reshape([-1 if axis == axis_at else 1 for axis in range(values.ndim)]) for axis_at in (source, target)]
    chosen = jax.random.permutation(rng, blocks)[partner]
    strong = (owner == chosen) | (owner == (partner + blocks // 2) % blocks)
    return jnp.where(strong, factor * values, values)


def steps_of(key, dims, shards, low, high):
    def one(dim, shards_of):
        steps = jax.random.uniform(jax.random.fold_in(jax.random.fold_in(key, 6), dim), (shards_of,), jnp.float32, low / len(shards), high / len(shards))
        return jnp.repeat(jnp.exp(steps), dims[dim] // shards_of).reshape((-1,) + (1,) * (len(dims) - dim - 1))

    factor_of = one(*shards[0])
    for cut in shards[1:]:
        factor_of = factor_of * one(*cut)
    return factor_of


def noise(key, shape, width, limit, shards=(), kind=jnp.bfloat16):
    loudness = steps_of(key, shape, shards, -0.22, 0.18) if shards else 1.0
    result = jax.random.normal(key, shape, jnp.float32) * width * loudness
    return jnp.minimum(jnp.maximum(result, -limit), limit).astype(kind)


def gaussian_with(rng, extent, width, bound, cuts, heavy, kind=jnp.bfloat16):
    result = width * jax.random.normal(rng, extent, jnp.float32)
    if cuts:
        result = result * steps_of(rng, extent, cuts, -0.22, 0.18)
    return jnp.clip(raised(result, jax.random.fold_in(rng, 3), *heavy), -bound, bound).astype(kind)


def setup_inputs(seed: int = 0) -> dict:
    keys = jax.random.split(jax.random.key(seed), 5)
    cotangent = gaussian_with(keys[0], (TOKENS, D), 1.0, 6.0, ((0, 16),), (0, 1, 16, 2.0))
    gate_pre = noise(keys[1], (TOKENS, FF), 1.0, 6.0, ((0, 16), (1, 2)))
    up_pre = noise(keys[2], (TOKENS, FF), 1.0, 6.0, ((0, 16), (1, 2)))
    w_down = noise(keys[3], (D, FF), FF ** -0.5, 0.046875, ((0, 16), (1, 2)))
    return dict(cotangent=cotangent, gate_pre=gate_pre, up_pre=up_pre, w_down=w_down)


def reference(cotangent, gate_pre, up_pre, w_down):
    gate_wide = gate_pre.astype(jnp.float32)
    up_wide = up_pre.astype(jnp.float32)
    sigmoid_gate = 1.0 / (1.0 + jnp.exp(-gate_wide))
    activated = gate_wide * sigmoid_gate
    hidden = (activated * up_wide).astype(jnp.bfloat16)
    grad_hidden = jnp.dot(cotangent, w_down, preferred_element_type=jnp.float32)
    grad_gate = (grad_hidden * up_wide * sigmoid_gate * (1.0 + gate_wide * (1.0 - sigmoid_gate))).astype(jnp.bfloat16)
    grad_up = (grad_hidden * activated).astype(jnp.bfloat16)
    cot_groups = cotangent.reshape(GROUPS, ROWS, D)
    hid_groups = hidden.reshape(GROUPS, ROWS, FF)

    def accumulate(running, pair):
        cot_block, hid_block = pair
        partial_value = jnp.dot(cot_block.T, hid_block, preferred_element_type=jnp.float32).astype(jnp.bfloat16)
        return running + partial_value.astype(jnp.float32), None

    summed, _ = lax.scan(accumulate, jnp.zeros((D, FF), jnp.float32), (cot_groups, hid_groups))
    grad_down = (summed / GROUPS).astype(jnp.bfloat16)
    return grad_gate, grad_up, grad_down
```

```python
import jax
import jax.numpy as jnp
from jax import lax
from jax.sharding import PartitionSpec as P

together = lax.optimization_barrier


def swap(value, distance):
    pairs = [(at, at ^ distance) for at in range(lax.axis_size("dp"))]
    return lax.ppermute(value, "dp", pairs)


def wide(value):
    return value.astype(jnp.float32)


class Gather:
    def __init__(self, value):
        self.own, self.up, self.down = value, [value], [value]

    def step(self):
        size, step = lax.axis_size("ctx"), len(self.up)
        up = lax.ppermute(self.up[-1], "ctx", [(k, k + 1) for k in range(step - 1, size - 1)])
        down = lax.ppermute(self.down[-1], "ctx", [(k, k - 1) for k in range(1, size - step + 1)])
        return [up, down]

    def keep(self, arrived):
        self.up.append(arrived[0])
        self.down.append(arrived[1])

    def whole(self):
        size, at = lax.axis_size("ctx"), lax.axis_index("ctx")
        return jnp.concatenate(
            [self.own]
            + [jnp.where(at >= j, self.up[j], self.down[size - j]) for j in range(1, size)]
        )


class Scatter:
    def __init__(self, partial):
        self.partial, self.arrived, self.count = partial, None, 0

    def block(self, target):
        size = lax.axis_size("ctx")
        rows = self.partial.shape[0] // size
        start = jnp.clip(target, 0, size - 1) * rows
        return lax.dynamic_slice_in_dim(self.partial, start, rows, 0)

    def step(self):
        size, at = lax.axis_size("ctx"), lax.axis_index("ctx")
        self.count += 1
        step = self.count
        up, down = self.block(at + size - step), self.block(at - size + step)
        if step > 1:
            up, down = up + self.arrived[0], down + self.arrived[1]
        return [
            lax.ppermute(up, "ctx", [(k, k + 1) for k in range(step)]),
            lax.ppermute(down, "ctx", [(size - 1 - k, size - 2 - k) for k in range(step)]),
        ]

    def keep(self, arrived):
        self.arrived = arrived

    def total(self):
        return (
            wide(self.block(lax.axis_index("ctx")))
            + wide(self.arrived[0])
            + wide(self.arrived[1])
        )


def send_first(partial):
    rows = partial.shape[0] // 4
    half = rows // 2
    for_x, for_y, across = [partial[k * rows : (k + 1) * rows] for k in (1, 2, 3)]
    return [
        swap(across[:half], 1),
        swap(across[half:], 2),
        swap(for_x[:half], 1),
        swap(for_y[half:], 2),
    ]


def send_second(partial, first):
    rows = partial.shape[0] // 4
    half = rows // 2
    return [
        swap(partial[rows + half : 2 * rows] + first[1], 1),
        swap(partial[2 * rows : 2 * rows + half] + first[0], 2),
    ]


def sum_plane(partial, first, second):
    rows = partial.shape[0] // 4
    half = rows // 2
    return jnp.concatenate(
        [
            wide(partial[:half]) + wide(first[2]) + wide(second[1]),
            wide(partial[half:rows]) + wide(second[0]) + wide(first[3]),
        ]
    )


def local(cotangent, gate_pre, up_pre, w_down):
    groups = lax.axis_size(("dp", "ctx"))
    size, at = lax.axis_size("ctx"), lax.axis_index("ctx")
    width = gate_pre.shape[1] // 2
    owned = cotangent.shape[1] // lax.axis_size("dp")
    small = owned // size
    half = cotangent.shape[0] // 2
    me = lax.axis_index("dp")
    cuts = (slice(0, width), slice(width, 2 * width))

    def features(k):
        return lax.dynamic_slice_in_dim(cotangent, (me ^ k) * owned, owned, 1)

    def activation(cut):
        gate = wide(gate_pre[:, cut])
        return (gate * jax.nn.sigmoid(gate) * wide(up_pre[:, cut])).astype(jnp.bfloat16)

    def weight_dot(gathered):
        return jnp.dot(turned, gathered.whole(), preferred_element_type=jnp.float32).astype(
            jnp.bfloat16
        )

    def down_dot(parts):
        return lax.dot_general(
            block,
            jnp.concatenate(parts),
            (((0,), (0,)), ((), ())),
            preferred_element_type=jnp.float32,
        ).astype(jnp.bfloat16)

    def finish(cut, grad_hidden):
        gate, up = wide(gate_pre[:, cut]), wide(up_pre[:, cut])
        s = jax.nn.sigmoid(gate)
        return (
            (grad_hidden * up * s * (1.0 + gate * (1.0 - s))).astype(jnp.bfloat16),
            (grad_hidden * (gate * s)).astype(jnp.bfloat16),
        )

    g0, g1 = Gather(w_down[:, cuts[0]]), Gather(w_down[:, cuts[1]])
    h0 = activation(cuts[0])
    a, b, c, x0, h1 = together(
        (
            g0.step(),
            g1.step(),
            [features(0)] + [swap(features(k), k) for k in (1, 2, 3)],
            [swap(h0, 1), swap(h0, 2)],
            activation(cuts[1]),
        )
    )
    g0.keep(a)
    g1.keep(b)
    block = jnp.concatenate(c)
    turned = jnp.concatenate(
        [
            lax.dynamic_slice_in_dim(block, lax.rem(at - j + size, size) * small, small, 1)
            for j in range(size)
        ],
        axis=1,
    )
    a, b, y0, x1 = together(
        (
            g0.step(),
            g1.step(),
            [swap(x0[1][:half], 1), swap(x0[0][half:], 2)],
            [swap(h1, 1), swap(h1, 2)],
        )
    )
    g0.keep(a)
    g1.keep(b)
    a, y1, d0 = together(
        (
            g0.step(),
            [swap(x1[1][:half], 1), swap(x1[0][half:], 2)],
            down_dot([h0] + x0 + y0),
        )
    )
    g0.keep(a)
    s0 = Scatter(d0)
    a, b, p0, d1 = together(
        (s0.step(), g1.step(), weight_dot(g0), down_dot([h1] + x1 + y1))
    )
    s0.keep(a)
    g1.keep(b)
    s1 = Scatter(d1)
    a, b, f0, p1 = together((s0.step(), s1.step(), send_first(p0), weight_dot(g1)))
    s0.keep(a)
    s1.keep(b)
    a, b, e0, f1 = together((s0.step(), s1.step(), send_second(p0, f0), send_first(p1)))
    s0.keep(a)
    s1.keep(b)
    a, e1, o0 = together(
        (s1.step(), send_second(p1, f1), finish(cuts[0], sum_plane(p0, f0, e0)))
    )
    s1.keep(a)
    o1 = finish(cuts[1], sum_plane(p1, f1, e1))
    down = [(s.total() / groups).astype(jnp.bfloat16) for s in (s0, s1)]
    return (
        jnp.concatenate([o0[0], o1[0]], axis=1),
        jnp.concatenate([o0[1], o1[1]], axis=1),
        jnp.concatenate(down, axis=1),
    )


def solution(mesh):
    in_specs = (
        P(("dp", "ctx"), None),
        P(("dp", "ctx"), "tp"),
        P(("dp", "ctx"), "tp"),
        P(("dp", "ctx"), "tp"),
    )
    out_specs = (P(("dp", "ctx"), "tp"), P(("dp", "ctx"), "tp"), P(("dp", "ctx"), "tp"))
    return jax.shard_map(local, mesh=mesh, in_specs=in_specs, out_specs=out_specs, check_vma=False)
```

```python
import jax
import jax.numpy as jnp
from jax import lax
from jax.sharding import PartitionSpec as P

together = lax.optimization_barrier


def swap(value, distance):
    pairs = [(at, at ^ distance) for at in range(lax.axis_size("dp"))]
    return lax.ppermute(value, "dp", pairs)


def wide(value):
    return value.astype(jnp.float32)


class Gather:
    def __init__(self, value):
        self.own, self.up, self.down = value, [value], [value]

    def step(self):
        size, step = lax.axis_size("ctx"), len(self.up)
        up = lax.ppermute(self.up[-1], "ctx", [(k, k + 1) for k in range(step - 1, size - 1)])
        down = lax.ppermute(self.down[-1], "ctx", [(k, k - 1) for k in range(1, size - step + 1)])
        return [up, down]

    def keep(self, arrived):
        self.up.append(arrived[0])
        self.down.append(arrived[1])

    def whole(self):
        size, at = lax.axis_size("ctx"), lax.axis_index("ctx")
        return jnp.concatenate(
            [self.own]
            + [jnp.where(at >= j, self.up[j], self.down[size - j]) for j in range(1, size)]
        )


class Scatter:
    def __init__(self, partial):
        self.partial, self.arrived, self.count = partial, None, 0

    def block(self, target):
        size = lax.axis_size("ctx")
        rows = self.partial.shape[0] // size
        start = jnp.clip(target, 0, size - 1) * rows
        return lax.dynamic_slice_in_dim(self.partial, start, rows, 0)

    def blocks(self):
        size, at = lax.axis_size("ctx"), lax.axis_index("ctx")
        self.count += 1
        step = self.count
        up, down = self.block(at + size - step), self.block(at - size + step)
        if step > 1:
            up, down = up + self.arrived[0], down + self.arrived[1]
        return up, down

    def push(self, value, step, way):
        last = lax.axis_size("ctx") - 1
        pairs = [(k, k + 1) if way > 0 else (last - k, last - 1 - k) for k in range(step)]
        return lax.ppermute(value, "ctx", pairs)

    def step(self):
        up, down = self.blocks()
        return [self.push(up, self.count, 1), self.push(down, self.count, -1)]

    def keep(self, arrived):
        self.arrived = arrived

    def total(self):
        return (
            wide(self.block(lax.axis_index("ctx")))
            + wide(self.arrived[0])
            + wide(self.arrived[1])
        )


def first_parts(partial):
    rows = partial.shape[0] // 4
    half = rows // 2
    for_x, for_y, across = [partial[k * rows : (k + 1) * rows] for k in (1, 2, 3)]
    return (
        jnp.concatenate([across[:half], for_x[:half]]),
        jnp.concatenate([across[half:], for_y[half:]]),
    )


def second_parts(partial, first):
    rows = partial.shape[0] // 4
    half = rows // 2
    return (
        partial[rows + half : 2 * rows] + first[1][:half],
        partial[2 * rows : 2 * rows + half] + first[0][:half],
    )


def swap_both(parts):
    return [swap(parts[0], 1), swap(parts[1], 2)]


def send_first(partial):
    return swap_both(first_parts(partial))


def send_second(partial, first):
    return swap_both(second_parts(partial, first))


def both_sends(old, old_first, new):
    half = old.shape[0] // 8
    second, first = second_parts(old, old_first), first_parts(new)
    sent = swap_both([jnp.concatenate([one, two]) for one, two in zip(second, first)])
    return [one[:half] for one in sent], [one[half:] for one in sent]


def both_steps(older, newer):
    (up, down), (next_up, next_down) = older.blocks(), newer.blocks()
    rows = up.shape[0]
    step = older.count
    up = older.push(jnp.concatenate([up, next_up]), step, 1)
    down = older.push(jnp.concatenate([down, next_down]), step, -1)
    return [up[:rows], down[:rows]], [up[rows:], down[rows:]]


def sum_plane(partial, first, second):
    rows = partial.shape[0] // 4
    half = rows // 2
    return jnp.concatenate(
        [
            wide(partial[:half]) + wide(first[0][half:]) + wide(second[1]),
            wide(partial[half:rows]) + wide(second[0]) + wide(first[1][half:]),
        ]
    )


def local(cotangent, gate_pre, up_pre, w_down):
    groups = lax.axis_size(("dp", "ctx"))
    size, at = lax.axis_size("ctx"), lax.axis_index("ctx")
    width = gate_pre.shape[1] // 2
    owned = cotangent.shape[1] // lax.axis_size("dp")
    small = owned // size
    half = cotangent.shape[0] // 2
    me = lax.axis_index("dp")
    cuts = (slice(0, width), slice(width, 2 * width))

    def features(k):
        return lax.dynamic_slice_in_dim(cotangent, (me ^ k) * owned, owned, 1)

    def activation(cut):
        gate = wide(gate_pre[:, cut])
        return (gate * jax.nn.sigmoid(gate) * wide(up_pre[:, cut])).astype(jnp.bfloat16)

    def weight_dot(gathered):
        return jnp.dot(turned, gathered, preferred_element_type=jnp.float32).astype(
            jnp.bfloat16
        )

    def down_dot(parts):
        return lax.dot_general(
            block,
            jnp.concatenate(parts),
            (((0,), (0,)), ((), ())),
            preferred_element_type=jnp.float32,
        ).astype(jnp.bfloat16)

    def finish(cut, grad_hidden):
        gate, up = wide(gate_pre[:, cut]), wide(up_pre[:, cut])
        s = jax.nn.sigmoid(gate)
        return (
            (grad_hidden * up * s * (1.0 + gate * (1.0 - s))).astype(jnp.bfloat16),
            (grad_hidden * (gate * s)).astype(jnp.bfloat16),
        )

    gathered = Gather(w_down)
    h0 = activation(cuts[0])
    a, x0, far, h1 = together(
        (
            gathered.step(),
            [swap(jnp.concatenate([h0, features(k)], axis=1), k) for k in (1, 2)],
            swap(features(3), 3),
            activation(cuts[1]),
        )
    )
    gathered.keep(a)
    block = jnp.concatenate([features(0), x0[0][:, width:], x0[1][:, width:], far])
    x0 = [x0[0][:, :width], x0[1][:, :width]]
    turned = jnp.concatenate(
        [
            lax.dynamic_slice_in_dim(block, lax.rem(at - j + size, size) * small, small, 1)
            for j in range(size)
        ],
        axis=1,
    )
    a, x1 = together(
        (
            gathered.step(),
            [
                swap(jnp.concatenate([x0[1][:half], h1]), 1),
                swap(jnp.concatenate([x0[0][half:], h1]), 2),
            ],
        )
    )
    gathered.keep(a)
    y0 = [x1[0][:half], x1[1][:half]]
    x1 = [x1[0][half:], x1[1][half:]]
    s0 = Scatter(down_dot([h0] + x0 + y0))
    a, y1, b = together(
        (
            gathered.step(),
            [swap(x1[1][:half], 1), swap(x1[0][half:], 2)],
            s0.step(),
        )
    )
    gathered.keep(a)
    s0.keep(b)
    weights = gathered.whole()
    p0 = weight_dot(weights[:, cuts[0]])
    s1 = Scatter(down_dot([h1] + x1 + y1))
    a, b, f0, p1 = together(
        (s0.step(), s1.step(), send_first(p0), weight_dot(weights[:, cuts[1]]))
    )
    s0.keep(a)
    s1.keep(b)
    a, b, e0, f1 = together(both_steps(s0, s1) + both_sends(p0, f0, p1))
    s0.keep(a)
    s1.keep(b)
    a, e1, o0 = together(
        (s1.step(), send_second(p1, f1), finish(cuts[0], sum_plane(p0, f0, e0)))
    )
    s1.keep(a)
    o1 = finish(cuts[1], sum_plane(p1, f1, e1))
    down = [(s.total() / groups).astype(jnp.bfloat16) for s in (s0, s1)]
    return (
        jnp.concatenate([o0[0], o1[0]], axis=1),
        jnp.concatenate([o0[1], o1[1]], axis=1),
        jnp.concatenate(down, axis=1),
    )


def solution(mesh):
    in_specs = (
        P(("dp", "ctx"), None),
        P(("dp", "ctx"), "tp"),
        P(("dp", "ctx"), "tp"),
        P(("dp", "ctx"), "tp"),
    )
    out_specs = (P(("dp", "ctx"), "tp"), P(("dp", "ctx"), "tp"), P(("dp", "ctx"), "tp"))
    return jax.shard_map(local, mesh=mesh, in_specs=in_specs, out_specs=out_specs, check_vma=False)
```
